32 devices in a mesh: seq: 8 (over z, x), fsdp: 4 (over y, core).
Axes of the slice: x: 2, y: 2, z: 4, core: 2. Of those that a mesh axis runs over, the one named last changes fastest.
Arguments:
- hidden_in: bfloat16 [4, 2048, 1024], P('fsdp', 'seq'), may hold values from -24 to 24
- cotangent: float32 [4, 2048, 1024], P('fsdp', 'seq'), may hold values from -6 to 6
- gains: float32 [2, 3072], P(None, 'fsdp'), may hold values from 0.5 to 1.5
- gains_first: float32 [2, 3072], P(None, 'fsdp'), may hold values from -64 to 64
- gains_second: float32 [2, 3072], P(None, 'fsdp'), may hold values from 245.76 to 2457.6
- in_proj: float32 [2, 1024, 4384], P(None, 'fsdp'), may hold values from -0.1875 to 0.1875
- in_proj_first: float32 [2, 1024, 4384], P(None, 'fsdp'), may hold values from -32 to 32
- in_proj_second: float32 [2, 1024, 4384], P(None, 'fsdp'), may hold values from 61.44 to 614.4
- conv_taps: float32 [2, 5, 2304], P(None, None, 'fsdp'), may hold values from -3 to 3
- conv_taps_first: float32 [2, 5, 2304], P(None, None, 'fsdp'), may hold values from -32 to 32
- conv_taps_second: float32 [2, 5, 2304], P(None, None, 'fsdp'), may hold values from 61.44 to 614.4
- head_params: float32 [2, 3, 32], P(None, None, 'fsdp'), may hold values from -9 to 1.5
- head_params_first: float32 [2, 3, 32], P(None, None, 'fsdp'), may hold values from -192 to 192
- head_params_second: float32 [2, 3, 32], P(None, None, 'fsdp'), may hold values from 2211.84 to 22118.4
- out_proj: float32 [2, 2048, 1024], P(None, 'fsdp'), may hold values from -0.125 to 0.125
- out_proj_first: float32 [2, 2048, 1024], P(None, 'fsdp'), may hold values from -64 to 64
- out_proj_second: float32 [2, 2048, 1024], P(None, 'fsdp'), may hold values from 245.76 to 2457.6
Outputs:
- hidden_out: float32 [4, 2048, 1024], P('fsdp', 'seq')
- hidden_grad: float32 [4, 2048, 1024], P('fsdp', 'seq')
- gains_first_new: float32 [2, 3072], P(None, 'fsdp')
- gains_second_new: float32 [2, 3072], P(None, 'fsdp')
- gains_new: float32 [2, 3072], P(None, 'fsdp')
- in_proj_first_new: float32 [2, 1024, 4384], P(None, 'fsdp')
- in_proj_second_new: float32 [2, 1024, 4384], P(None, 'fsdp')
- in_proj_new: float32 [2, 1024, 4384], P(None, 'fsdp')
- conv_taps_first_new: float32 [2, 5, 2304], P(None, None, 'fsdp')
- conv_taps_second_new: float32 [2, 5, 2304], P(None, None, 'fsdp')
- conv_taps_new: float32 [2, 5, 2304], P(None, None, 'fsdp')
- head_params_first_new: float32 [2, 3, 32], P(None, None, 'fsdp')
- head_params_second_new: float32 [2, 3, 32], P(None, None, 'fsdp')
- head_params_new: float32 [2, 3, 32], P(None, None, 'fsdp')
- out_proj_first_new: float32 [2, 2048, 1024], P(None, 'fsdp')
- out_proj_second_new: float32 [2, 2048, 1024], P(None, 'fsdp')
- out_proj_new: float32 [2, 2048, 1024], P(None, 'fsdp')
The draws below stay inside these ranges and needn't reach their ends.
All inputs are finite; a program needn't handle non-finite values.
Results may differ from the reference program's by a relative error of at most 0.025.
The reference program's roundings to bfloat16 on the way count: a program that leaves them out, or rounds other values in their place, can miss the bound.
Values may be sent and summed in bfloat16 or wider, within the bound.
A program may use at most 320 MiB of HBM per device.

```python
import math
import jax
import jax.numpy as jnp
from jax import lax

D = 1024
H = 32
P_SIZE = 64
STATE = 128
TAPS = 4
SPAN = 256
LAYERS = 2
STEP = 10
DI = 2048
CH = 2304
E = 4384
GAINS = 3072
LEN = 2048
NSEQ = 4
TOKENS = 8192


def draw_hidden_in(key, part):
    key = jax.random.fold_in(key, 11)
    keys = jax.random.split(key, 3)
    values = jax.random.truncated_normal(keys[0], -4.0, 4.0, (NSEQ, LEN, D), jnp.float32)
    row_scale = jnp.exp(jax.random.uniform(keys[1], (NSEQ, LEN, 1), jnp.float32, math.log(0.3), math.log(3.0)))
    column_scale = jnp.exp(jax.random.uniform(keys[2], (1, 1, D), jnp.float32, math.log(0.5), math.log(2.0)))
    return (values * row_scale * column_scale).astype(jnp.bfloat16)


def draw_head_params(key, part):
    key = jax.random.fold_in(key, 23)
    keys = jax.random.split(key, 4)
    selector = jax.random.uniform(keys[0], (LAYERS, H), jnp.float32)
    slow_rate = jnp.exp(jax.random.uniform(keys[1], (LAYERS, H), jnp.float32, math.log(0.2 / LEN), math.log(2.0 / LEN)))
    fast_rate = jnp.exp(jax.random.uniform(keys[2], (LAYERS, H), jnp.float32, math.log(2.0 / LEN), math.log(1.0 / 30.0)))
    slow_share = 0.5
    decay_rate = jnp.where(selector < slow_share, slow_rate, fast_rate)
    step_target = 0.3 * jnp.sqrt(decay_rate)
    step_bias = jnp.log(step_target) - 0.5
    log_rate = jnp.log(decay_rate / step_target)
    skip_gain = jax.random.uniform(keys[3], (LAYERS, H), jnp.float32, 0.5, 1.5)
    return jnp.stack([step_bias, log_rate, skip_gain], axis=1)


def block_levels(own_key, shape, shards, least, high):
    gain = 1.0
    for position, shards_of in shards:
        heights = jax.random.uniform(jax.random.fold_in(jax.random.fold_in(own_key, 6), position), (shards_of,), jnp.float32, least / len(shards), high / len(shards))
        gain = gain * jnp.repeat(jnp.exp(heights), shape[position] // shards_of).reshape((-1,) + (1,) * (len(shape) - 1 - position))
    return gain


def normal_values(key, shape, scale, bound, shards=(), dtype=jnp.bfloat16):
    level = block_levels(key, shape, shards, -0.22, 0.18) if shards else 1.0
    entries = jax.random.normal(key, shape, jnp.float32) * scale * level
    return jnp.minimum(jnp.maximum(entries, -bound), bound).astype(dtype)


def setup_inputs(seed: int = 0) -> dict:
    key_of = jax.random.split(jax.random.key(seed), 18)
    return {
        "hidden_in": draw_hidden_in(jax.random.fold_in(key_of[17], 71), 0),
        "cotangent": normal_values(key_of[1], (NSEQ, LEN, D), 1.0, 6.0, ((0, 4), (1, 8)), jnp.float32),
        "gains": jnp.clip(1.0 + 0.1 * jax.random.normal(key_of[2], (LAYERS, GAINS), jnp.float32), 0.5, 1.5),
        "gains_first": normal_values(key_of[3], (LAYERS, GAINS), (0.11 * TOKENS ** 0.5), 64.0, ((1, 4),), jnp.float32),
        "gains_second": jnp.clip(jnp.exp(math.log(2457.6) - 2.3025852 * jax.random.uniform(key_of[4], (LAYERS, GAINS), jnp.float32) ** block_levels(key_of[4], (LAYERS, GAINS), ((1, 4),), -0.2, 0.2)), 245.76, 2457.6),
        "in_proj": normal_values(key_of[5], (LAYERS, D, E), D ** -0.5, 0.1875, ((1, 4),), jnp.float32),
        "in_proj_first": normal_values(key_of[6], (LAYERS, D, E), (0.055 * TOKENS ** 0.5), 32.0, ((1, 4),), jnp.float32),
        "in_proj_second": jnp.clip(jnp.exp(math.log(614.4) - 2.3025852 * jax.random.uniform(key_of[7], (LAYERS, D, E), jnp.float32) ** block_levels(key_of[7], (LAYERS, D, E), ((1, 4),), -0.2, 0.2)), 61.44, 614.4),
        "conv_taps": normal_values(key_of[8], (LAYERS, TAPS + 1, CH), TAPS ** -0.5, 3.0, ((2, 4),), jnp.float32),
        "conv_taps_first": normal_values(key_of[9], (LAYERS, TAPS + 1, CH), (0.055 * TOKENS ** 0.5), 32.0, ((2, 4),), jnp.float32),
        "conv_taps_second": jnp.clip(jnp.exp(math.log(614.4) - 2.3025852 * jax.random.uniform(key_of[10], (LAYERS, TAPS + 1, CH), jnp.float32) ** block_levels(key_of[10], (LAYERS, TAPS + 1, CH), ((2, 4),), -0.2, 0.2)), 61.44, 614.4),
        "head_params": draw_head_params(jax.random.fold_in(key_of[17], 71), 0),
        "head_params_first": normal_values(key_of[12], (LAYERS, 3, H), (0.33 * TOKENS ** 0.5), 192.0, ((2, 4),), jnp.float32),
        "head_params_second": jnp.clip(jnp.exp(math.log(22118.4) - 2.3025851 * jax.random.uniform(key_of[13], (LAYERS, 3, H), jnp.float32) ** block_levels(key_of[13], (LAYERS, 3, H), ((2, 4),), -0.2, 0.2)), 2211.84, 22118.4),
        "out_proj": normal_values(key_of[14], (LAYERS, DI, D), DI ** -0.5, 0.125, ((1, 4),), jnp.float32),
        "out_proj_first": normal_values(key_of[15], (LAYERS, DI, D), (0.11 * TOKENS ** 0.5), 64.0, ((1, 4),), jnp.float32),
        "out_proj_second": jnp.clip(jnp.exp(math.log(2457.6) - 2.3025852 * jax.random.uniform(key_of[16], (LAYERS, DI, D), jnp.float32) ** block_levels(key_of[16], (LAYERS, DI, D), ((1, 4),), -0.2, 0.2)), 245.76, 2457.6),
    }


highest = lax.Precision.HIGHEST
norm_eps = 1e-05
beta_one = 0.9
beta_two = 0.95
adam_eps = 1e-08
learn_rates = (0.4, 0.06, 0.5, 3.0, 0.05)
weight_decays = (0.0, 0.1, 0.0, 0.0, 0.1)

@jax.custom_vjp
def low(v):
    return lax.optimization_barrier(v.astype(jnp.bfloat16)).astype(jnp.float32)

@jax.custom_vjp
def low_back(v):
    return v

def low_keep(v):
    return (low(v), None)

def low_pass(kept, grad):
    return (grad,)

def back_keep(v):
    return (v, None)

def back_low(kept, grad):
    return (low(grad),)
low.defvjp(low_keep, low_pass)
low_back.defvjp(back_keep, back_low)

def rms_norm(values, gain_vec):
    mean_sq = lax.optimization_barrier(jnp.mean(values * values, axis=-1, keepdims=True))
    return values * lax.rsqrt(mean_sq + norm_eps) * gain_vec

def causal_conv(signal, taps_bias, rim_vals):
    padded = jnp.concatenate([rim_vals, signal], axis=1)
    tap_count = taps_bias.shape[0] - 1
    tok_count = signal.shape[1]
    summed = jnp.zeros_like(signal) + taps_bias[tap_count]
    for tap_idx in range(tap_count):
        summed = summed + padded[:, tap_idx:tap_idx + tok_count, :] * taps_bias[tap_idx]
    return jax.nn.silu(summed)

def ssd_blocks(x_heads, step_size, log_decay, b_state, c_state):
    tok_count, head_count, head_width = x_heads.shape
    states = b_state.shape[1]
    groups = tok_count // SPAN
    positions = jnp.arange(SPAN)
    causal = (positions[:, None] >= positions[None, :]).astype(jnp.float32)

    def one_block(state_carry, block_items):
        x_blk, step_blk, decay_blk, b_blk, c_blk = block_items
        cumulative = jnp.cumsum(decay_blk, axis=0)
        log_gaps = cumulative[:, None, :] - cumulative[None, :, :]
        kernel = jnp.exp(log_gaps * causal[:, :, None]) * causal[:, :, None]
        inner_prod = jnp.dot(c_blk, b_blk.T, precision=highest)
        mixing = kernel * inner_prod[:, :, None] * step_blk[None, :, :]
        within = jnp.einsum('tsh,shp->thp', mixing, x_blk, precision=highest)
        from_carry = jnp.exp(cumulative)[:, :, None] * jnp.einsum('tn,hpn->thp', c_blk, state_carry, precision=highest)
        tail_weight = jnp.exp(cumulative[-1][None, :] - cumulative) * step_blk
        carry_next = jnp.exp(cumulative[-1])[:, None, None] * state_carry + jnp.einsum('shp,sn->hpn', x_blk * tail_weight[:, :, None], b_blk, precision=highest)
        return (carry_next, within + from_carry)
    block_items = (x_heads.reshape(groups, SPAN, head_count, head_width), step_size.reshape(groups, SPAN, head_count), log_decay.reshape(groups, SPAN, head_count), b_state.reshape(groups, SPAN, states), c_state.reshape(groups, SPAN, states))
    state_start = jnp.zeros((head_count, head_width, states), jnp.float32)
    final_state, outputs = lax.scan(jax.checkpoint(one_block), state_start, block_items)
    return (outputs.reshape(tok_count, head_count, head_width), final_state, lax.optimization_barrier(jnp.sum(log_decay, axis=0)))

def layer_forward(hidden, layer_weights):
    gain_vals, in_mat, conv_vals, head_vals, out_mat = layer_weights
    tok_count = hidden.shape[0]
    normed = low(rms_norm(hidden, gain_vals[:D]))
    projected = low_back(low(jnp.dot(normed, in_mat, precision=highest)))
    gate_cols = projected[:, :DI]
    conv_in = projected[:, DI:DI + CH]
    step_raw = projected[:, DI + CH:]
    rim_vals = jnp.zeros((1, TAPS - 1, CH), jnp.float32)
    conv_out = low(causal_conv(conv_in[None], conv_vals, rim_vals)[0])
    x_heads = conv_out[:, :DI].reshape(tok_count, H, P_SIZE)
    step_size = jax.nn.softplus(step_raw + head_vals[0])
    log_decay = -jnp.exp(head_vals[1]) * step_size
    mixed_out, final_state, totals = ssd_blocks(x_heads, step_size, log_decay, conv_out[:, DI:DI + STATE], conv_out[:, DI + STATE:])
    mixed_out = mixed_out + head_vals[2][None, :, None] * x_heads
    mixed_out = low_back(low(mixed_out.reshape(tok_count, DI)))
    normed_gate = low(rms_norm(mixed_out * jax.nn.silu(gate_cols), gain_vals[D:]))
    branch = low_back(jnp.dot(normed_gate, out_mat, precision=highest))
    return hidden + branch

def model(hidden, weights):
    rounded_w = tuple((low(weight) for weight in weights))
    for layer_idx in range(LAYERS):
        hidden = layer_forward(hidden, tuple((weight[layer_idx] for weight in rounded_w)))
    return hidden

def adam_step(weight, first_old, second_old, grad_vals, learn_rate, decay_rate):
    first_new = beta_one * first_old + (1.0 - beta_one) * grad_vals
    second_new = beta_two * second_old + (1.0 - beta_two) * grad_vals * grad_vals
    first_hat = first_new / (1.0 - beta_one ** STEP)
    second_hat = second_new / (1.0 - beta_two ** STEP)
    weight_new = weight - learn_rate * (first_hat / (jnp.sqrt(second_hat) + adam_eps) + decay_rate * weight)
    return (first_new, second_new, weight_new)

def reference(hidden_in, cotangent, gains, gains_first, gains_second, in_proj, in_proj_first, in_proj_second, conv_taps, conv_taps_first, conv_taps_second, head_params, head_params_first, head_params_second, out_proj, out_proj_first, out_proj_second):
    weights = (gains, in_proj, conv_taps, head_params, out_proj)
    firsts = (gains_first, in_proj_first, conv_taps_first, head_params_first, out_proj_first)
    seconds = (gains_second, in_proj_second, conv_taps_second, head_params_second, out_proj_second)

    def per_sequence(grad_totals, seq_items):
        seq_hidden, seq_cot = seq_items
        seq_out, pull_back = jax.vjp(model, seq_hidden.astype(jnp.float32), weights)
        grad_hidden, grad_weights = pull_back(seq_cot)
        summed = tuple((total_grad + new_grad for total_grad, new_grad in zip(grad_totals, grad_weights)))
        return (summed, (seq_out, grad_hidden))
    zero_grads = tuple((jnp.zeros_like(weight) for weight in weights))
    grads, (hidden_out, hidden_grad) = lax.scan(per_sequence, zero_grads, (hidden_in, cotangent))
    results = [hidden_out, hidden_grad]
    for kind_idx in range(5):
        first_new, second_new, weight_new = adam_step(weights[kind_idx], firsts[kind_idx], seconds[kind_idx], grads[kind_idx], learn_rates[kind_idx], weight_decays[kind_idx])
        results.extend([first_new, second_new, weight_new])
    return (results[0], results[1], results[2], results[3], results[4], results[5], results[6], results[7], results[8], results[9], results[10], results[11], results[12], results[13], results[14], results[15], results[16])
```

```python
import functools

import jax
import jax.numpy as jnp
from jax import lax
from jax.experimental import pallas as pl
from jax.experimental.pallas import tpu as pltpu
from jax.sharding import PartitionSpec as P

D = 1024
H = 32
HP = 64
STATE = 128
TAPS = 4
SPAN = 256
LAYERS = 2
STEP = 10
DI = 2048
CH = 2304
GROUP = 8
COLS = GROUP * HP

highest = lax.Precision.HIGHEST
norm_eps = 1e-05
beta_one = 0.9
beta_two = 0.95
adam_eps = 1e-08
learn_rates = (0.4, 0.06, 0.5, 3.0, 0.05)
weight_decays = (0.0, 0.1, 0.0, 0.0, 0.1)
bf16 = jnp.bfloat16
f32 = jnp.float32


def dot(a, b, ca, cb):
    return lax.dot_general(a, b, (((ca,), (cb,)), ((), ())), preferred_element_type=f32)


def head(ref, j):
    return ref[:, j * HP : (j + 1) * HP]


def state_kernel(x_ref, b_ref, w_ref, s_ref):
    w = jnp.transpose(w_ref[0])
    for j in range(GROUP):
        wx = (head(x_ref, j).astype(f32) * w[:, j : j + 1]).astype(bf16)
        s_ref[0, j * HP : (j + 1) * HP, :] = dot(wx, b_ref[...], 0, 0).astype(bf16)


def decay(cum, cum_cols, j, causal):
    gaps = cum_cols[:, j : j + 1] - cum[j : j + 1, :]
    return jnp.exp(jnp.where(causal, gaps, -1e30))


def causal_mask():
    rows = lax.broadcasted_iota(jnp.int32, (SPAN, SPAN), 0)
    cols = lax.broadcasted_iota(jnp.int32, (SPAN, SPAN), 1)
    return rows >= cols


def inner_kernel(x_ref, b_ref, c_ref, cum_ref, dt_ref, y_ref):
    causal = causal_mask()
    cb = dot(c_ref[...], b_ref[...], 1, 1)
    cum = cum_ref[0]
    dt = dt_ref[0]
    cum_cols = jnp.transpose(cum)
    for j in range(GROUP):
        mix = decay(cum, cum_cols, j, causal) * cb * dt[j : j + 1, :]
        y_ref[:, j * HP : (j + 1) * HP] = dot(mix.astype(bf16), head(x_ref, j), 1, 0)


def carry_kernel(y_ref, x_ref, c_ref, cum_ref, skip_ref, hin_ref, out_ref):
    grow = jnp.transpose(jnp.exp(cum_ref[0]))
    skip = jnp.transpose(skip_ref[0])
    for j in range(GROUP):
        rows = slice(j * HP, (j + 1) * HP)
        from_carry = dot(c_ref[...], hin_ref[0, rows, :], 1, 1) * grow[:, j : j + 1]
        skipped = head(x_ref, j).astype(f32) * skip[:, j : j + 1]
        out_ref[:, rows] = (y_ref[:, rows] + from_carry + skipped).astype(bf16)


def back_state_kernel(gy_ref, c_ref, cum_ref, g_ref):
    grow = jnp.transpose(jnp.exp(cum_ref[0]))
    for j in range(GROUP):
        egy = (head(gy_ref, j).astype(f32) * grow[:, j : j + 1]).astype(bf16)
        g_ref[0, j * HP : (j + 1) * HP, :] = dot(egy, c_ref[...], 0, 0).astype(bf16)


def back_inner_kernel(
    x_ref, gy_ref, b_ref, c_ref, cum_ref, dt_ref, skip_ref,
    gx_ref, gcb_ref, row_ref, col_ref, gskip_ref,
):
    causal = causal_mask()
    cb = dot(c_ref[...], b_ref[...], 1, 1)
    cum = cum_ref[0]
    dt = dt_ref[0]
    cum_cols = jnp.transpose(cum)
    dt_cols = jnp.transpose(dt)
    skip = jnp.transpose(skip_ref[0])

    @pl.when(pl.program_id(1) == 0)
    def _():
        gcb_ref[...] = jnp.zeros_like(gcb_ref)

    total = jnp.zeros((SPAN, SPAN), f32)
    row_list, skip_list = [], []
    for j in range(GROUP):
        e = decay(cum, cum_cols, j, causal)
        x = head(x_ref, j)
        gy = head(gy_ref, j)
        rho = dot(gy, x, 1, 1)
        e_rho = e * rho
        kept = e_rho * dt[j : j + 1, :]
        total = total + kept
        row_list.append(jnp.sum(kept * cb, axis=1, keepdims=True))
        col_ref[0, j : j + 1, :] = jnp.sum(e_rho * cb, axis=0, keepdims=True)
        gx = dot((e * cb).astype(bf16), gy, 0, 0) * dt_cols[:, j : j + 1]
        gyf = gy.astype(f32)
        gx_ref[:, j * HP : (j + 1) * HP] = gx + gyf * skip[:, j : j + 1]
        skip_list.append(jnp.sum(gyf * x.astype(f32), axis=1, keepdims=True))
    gcb_ref[0] += total
    row_ref[0] = jnp.transpose(jnp.concatenate(row_list, axis=1))
    gskip_ref[0] = jnp.transpose(jnp.concatenate(skip_list, axis=1))


def back_carry_kernel(
    gxi_ref, x_ref, gy_ref, b_ref, c_ref, cum_ref, w_ref, hin_ref, gs_ref,
    gx_ref, gb_ref, gc_ref, carry_ref, dw_ref, cross_ref,
):
    @pl.when(pl.program_id(1) == 0)
    def _():
        gb_ref[...] = jnp.zeros_like(gb_ref)
        gc_ref[...] = jnp.zeros_like(gc_ref)

    grow = jnp.transpose(jnp.exp(cum_ref[0]))
    w = jnp.transpose(w_ref[0])
    gb = jnp.zeros((SPAN, STATE), f32)
    gc = jnp.zeros((SPAN, STATE), f32)
    carry_list, dw_list = [], []
    for j in range(GROUP):
        rows = slice(j * HP, (j + 1) * HP)
        hin = hin_ref[0, rows, :]
        gs = gs_ref[0, rows, :]
        x = head(x_ref, j).astype(f32)
        egy = head(gy_ref, j).astype(f32) * grow[:, j : j + 1]
        b_gs = dot(b_ref[...], gs, 1, 1)
        c_hin = dot(c_ref[...], hin, 1, 1)
        gx_ref[:, rows] = gxi_ref[:, rows] + b_gs * w[:, j : j + 1]
        dw_list.append(jnp.sum(x * b_gs, axis=1, keepdims=True))
        carry_list.append(jnp.sum(egy * c_hin, axis=1, keepdims=True))
        gb = gb + dot((x * w[:, j : j + 1]).astype(bf16), gs, 1, 0)
        gc = gc + dot(egy.astype(bf16), hin, 1, 0)
        cross_ref[0, j : j + 1, :] = jnp.sum(hin.astype(f32) * gs.astype(f32), axis=0, keepdims=True)
    gb_ref[...] += gb
    gc_ref[...] += gc
    carry_ref[0] = jnp.transpose(jnp.concatenate(carry_list, axis=1))
    dw_ref[0] = jnp.transpose(jnp.concatenate(dw_list, axis=1))


x_spec = pl.BlockSpec((SPAN, COLS), lambda g, i: (g, i))
b_spec = pl.BlockSpec((SPAN, STATE), lambda g, i: (g, DI // STATE))
c_spec = pl.BlockSpec((SPAN, STATE), lambda g, i: (g, DI // STATE + 1))
bc_out_spec = pl.BlockSpec((SPAN, STATE), lambda g, i: (g, 0))
row_spec = pl.BlockSpec((1, GROUP, SPAN), lambda g, i: (g, i, 0))
one_spec = pl.BlockSpec((1, GROUP, 1), lambda g, i: (0, i, 0))
state_spec = pl.BlockSpec((1, COLS, STATE), lambda g, i: (g, i, 0))
gcb_spec = pl.BlockSpec((1, SPAN, SPAN), lambda g, i: (g, 0, 0))
cross_spec = pl.BlockSpec((1, GROUP, STATE), lambda g, i: (g, i, 0))


def call(kernel, name, chunks, ins, outs, flops, *args):
    shapes = [s for _, s in outs]
    moved = sum(a.size * a.dtype.itemsize for a in args)
    moved += sum(s.size * s.dtype.itemsize for s in shapes)
    return pl.pallas_call(
        kernel,
        grid=(chunks, H // GROUP),
        in_specs=ins,
        out_specs=[s for s, _ in outs],
        out_shape=shapes,
        name=name,
        compiler_params=pltpu.CompilerParams(
            dimension_semantics=("arbitrary", "arbitrary"), vmem_limit_bytes=40 * 1024 * 1024
        ),
        cost_estimate=pl.CostEstimate(
            flops=flops * chunks, bytes_accessed=moved, transcendentals=chunks * H * SPAN * SPAN
        ),
    )(*args)


def shape(dims, dtype=f32):
    return jax.ShapeDtypeStruct(dims, dtype)


small_flops = 2 * SPAN * DI * STATE
inner_flops = 20 * H * SPAN * SPAN * HP


def rms_scale(values):
    return lax.rsqrt(jnp.mean(values * values, axis=-1, keepdims=True) + norm_eps)


def silu_slope(w):
    sig = jax.nn.sigmoid(w)
    return sig * (1.0 + w * (1.0 - sig))


def adam_step(weight, first_old, second_old, grad_vals, learn_rate, decay_rate):
    first_new = beta_one * first_old + (1.0 - beta_one) * grad_vals
    second_new = beta_two * second_old + (1.0 - beta_two) * grad_vals * grad_vals
    first_hat = first_new / (1.0 - beta_one**STEP)
    second_hat = second_new / (1.0 - beta_two**STEP)
    weight_new = weight - learn_rate * (
        first_hat / (jnp.sqrt(second_hat) + adam_eps) + decay_rate * weight
    )
    return (first_new, second_new, weight_new)


def exchange(states, seqs, weights, shards, spec):
    n = states.shape[0] // seqs
    own = DI // shards
    send = states.reshape(seqs * n, shards, own, STATE)
    got = lax.all_to_all(send, "seq", split_axis=1, concat_axis=0, tiled=False)
    got = got.reshape(shards, seqs, n, own // HP, HP * STATE)
    got = got.astype(f32)
    mixed = jnp.einsum(spec, weights, got, precision=highest).astype(bf16)
    mixed = mixed.reshape(shards, seqs * n, own, STATE)
    back = lax.all_to_all(mixed, "seq", split_axis=0, concat_axis=1, tiled=False)
    return back.reshape(seqs * n, DI, STATE)


def chunk_weights(totals, seqs, shards):
    n = totals.shape[0] // seqs
    every = lax.all_gather(totals.reshape(seqs, n, H), "seq", axis=1, tiled=True)
    chunks = shards * n
    own = H // shards
    mine = lax.dynamic_slice_in_dim(every, lax.axis_index("seq") * own, own, 2)
    place = jnp.arange(chunks)
    between = (place[None, None, :] < place[:, None, None]) & (place[None, None, :] > place[None, :, None])
    logs = jnp.einsum("ijk,bkh->ijbh", between.astype(f32), mine, precision=highest)
    ahead = (place[:, None] > place[None, :])[:, :, None, None]
    weights = jnp.where(ahead, jnp.exp(jnp.where(ahead, logs, 0.0)), 0.0)
    return weights.reshape(shards, n, shards, n, seqs, own)


def local(
    hidden_in,
    cotangent,
    gains,
    gains_first,
    gains_second,
    in_proj,
    in_proj_first,
    in_proj_second,
    conv_taps,
    conv_taps_first,
    conv_taps_second,
    head_params,
    head_params_first,
    head_params_second,
    out_proj,
    out_proj_first,
    out_proj_second,
):
    masters = (gains, in_proj, conv_taps, head_params, out_proj)
    firsts = (gains_first, in_proj_first, conv_taps_first, head_params_first, out_proj_first)
    seconds = (gains_second, in_proj_second, conv_taps_second, head_params_second, out_proj_second)
    shards = lax.axis_size("seq")
    owners = lax.axis_size("fsdp")
    fsdp_index = lax.axis_index("fsdp")
    seqs, toks, _ = hidden_in.shape
    rows = seqs * toks
    n = toks // SPAN
    chunks = seqs * n
    rim = TAPS - 1
    right = [(i, i + 1) for i in range(shards - 1)]
    left = [(i + 1, i) for i in range(shards - 1)]

    smalls = jnp.concatenate(
        [gains.reshape(-1), conv_taps.reshape(-1), head_params.reshape(-1)]
    ).astype(bf16)
    smalls = lax.all_gather(smalls, "fsdp", axis=0)
    size_a = gains.size
    size_b = size_a + conv_taps.size
    gains_all = smalls[:, :size_a].reshape(owners, LAYERS, -1)
    gains_all = jnp.moveaxis(gains_all, 0, 1).reshape(LAYERS, D + DI).astype(f32)
    taps_all = smalls[:, size_a:size_b].reshape(owners, LAYERS, TAPS + 1, -1)
    taps_all = jnp.moveaxis(taps_all, 0, 2).reshape(LAYERS, TAPS + 1, CH).astype(f32)
    heads_all = smalls[:, size_b:].reshape(owners, LAYERS, 3, -1)
    heads_all = jnp.moveaxis(heads_all, 0, 2).reshape(LAYERS, 3, H).astype(f32)
    in_mats = [
        lax.all_gather(in_proj[i].astype(bf16), "fsdp", axis=0, tiled=True) for i in range(LAYERS)
    ]
    out_mats = [
        lax.all_gather(out_proj[i].astype(bf16), "fsdp", axis=0, tiled=True) for i in range(LAYERS)
    ]

    upper = (jnp.arange(SPAN)[:, None] <= jnp.arange(SPAN)[None, :]).astype(f32)

    hidden = hidden_in.astype(f32).reshape(rows, D)
    saved = []
    for i in range(LAYERS):
        g1, g2 = gains_all[i, :D], gains_all[i, D:]
        taps, heads = taps_all[i], heads_all[i]
        rs1 = rms_scale(hidden)
        u = (hidden * rs1 * g1).astype(bf16)
        proj = dot(u, in_mats[i], 1, 0).astype(bf16)
        z = proj[:, :DI]
        c = proj[:, DI : DI + CH].reshape(seqs, toks, CH)
        raw = proj[:, DI + CH :].astype(f32).reshape(chunks, SPAN, H).transpose(0, 2, 1)
        halo = lax.ppermute(c[:, toks - rim :, :], "seq", right)
        padded = jnp.concatenate([halo, c], axis=1)
        pa = taps[TAPS]
        for k in range(TAPS):
            pa = pa + padded[:, k : k + toks, :].astype(f32) * taps[k]
        pa = pa.reshape(rows, CH)
        a = (pa * jax.nn.sigmoid(pa)).astype(bf16)
        pre = raw + heads[0][:, None]
        dt = jax.nn.softplus(pre)
        rate = -jnp.exp(heads[1])
        lam = rate[:, None] * dt
        cum = jnp.einsum("ghs,st->ght", lam, upper, precision=highest)
        last = cum[:, :, SPAN - 1 :]
        tail = jnp.exp(last - cum)
        w = tail * dt
        skip = heads[2].reshape(1, H, 1)
        (state,) = call(
            state_kernel, "chunk_state", chunks, [x_spec, b_spec, row_spec],
            [(state_spec, shape((chunks, DI, STATE), bf16))], small_flops, a, a, w,
        )
        weights = chunk_weights(last[:, :, 0], seqs, shards)
        hin = exchange(state, seqs, weights, shards, "imjnbh,jbnhx->ibmhx")
        (inner,) = call(
            inner_kernel, "inner", chunks, [x_spec, b_spec, c_spec, row_spec, row_spec],
            [(x_spec, shape((rows, DI)))], inner_flops // 3, a, a, a, cum, dt,
        )
        (y,) = call(
            carry_kernel, "carry", chunks,
            [x_spec, x_spec, c_spec, row_spec, one_spec, state_spec],
            [(x_spec, shape((rows, DI), bf16))], small_flops, inner, a, a, cum, skip, hin,
        )
        yf, zf = y.astype(f32), z.astype(f32)
        q = yf * (zf * jax.nn.sigmoid(zf))
        rs2 = rms_scale(q)
        nrm = (q * rs2 * g2).astype(bf16)
        saved.append((hidden, rs1, u, y, z, padded, pa, a, pre, dt, lam, rate, cum, last, w, skip, weights, hin, rs2, nrm))
        hidden = hidden + dot(nrm, out_mats[i], 1, 0)

    grad = cotangent.reshape(rows, D)
    big_grads = [None] * LAYERS
    small_grads = [None] * LAYERS
    for i in reversed(range(LAYERS)):
        (h, rs1, u, y, z, padded, pa, a, pre, dt, lam, rate, cum, last, w, skip, weights, hin, rs2, nrm) = saved[i]
        g1, g2 = gains_all[i, :D], gains_all[i, D:]
        taps = taps_all[i]
        go = grad.astype(bf16)
        gn = dot(go, out_mats[i], 1, 1)
        yf, zf = y.astype(f32), z.astype(f32)
        gate = zf * jax.nn.sigmoid(zf)
        q = yf * gate
        v = gn * g2
        gq = rs2 * v - q * (rs2 * rs2 * rs2) * jnp.mean(v * q, axis=-1, keepdims=True)
        grad_g2 = jnp.sum(gn * q * rs2, axis=0)
        gz = (gq * yf * silu_slope(zf)).astype(bf16)
        gy = (gq * gate).astype(bf16)
        (gstate,) = call(
            back_state_kernel, "back_state", chunks, [x_spec, c_spec, row_spec],
            [(state_spec, shape((chunks, DI, STATE), bf16))], small_flops, gy, a, cum,
        )
        gs = exchange(gstate, seqs, weights, shards, "imjnbh,ibmhx->jbnhx")
        grad_out = dot(nrm, go, 0, 0).astype(bf16)
        grad_out = lax.psum_scatter(grad_out, "fsdp", scatter_dimension=0, tiled=True)
        grad_out = lax.psum(grad_out, "seq").astype(f32)
        rows_shape = shape((chunks, H, SPAN))
        gx, gcb, row_pair, col_pair, gskip = call(
            back_inner_kernel, "back_inner", chunks,
            [x_spec, x_spec, b_spec, c_spec, row_spec, row_spec, one_spec],
            [
                (x_spec, shape((rows, DI))), (gcb_spec, shape((chunks, SPAN, SPAN))),
                (row_spec, rows_shape), (row_spec, rows_shape), (row_spec, rows_shape),
            ],
            inner_flops, a, gy, a, a, cum, dt, skip,
        )
        gx, gb, gc_state, carry, dw, cross = call(
            back_carry_kernel, "back_carry", chunks,
            [x_spec, x_spec, x_spec, b_spec, c_spec, row_spec, row_spec, state_spec, state_spec],
            [
                (x_spec, shape((rows, DI))), (bc_out_spec, shape((rows, STATE))),
                (bc_out_spec, shape((rows, STATE))), (row_spec, rows_shape), (row_spec, rows_shape),
                (cross_spec, shape((chunks, H, STATE))),
            ],
            4 * small_flops, gx, a, gy, a, a, cum, w, hin, gs,
        )
        gcb_b = gcb.astype(bf16)
        b_act = a[:, DI : DI + STATE].reshape(chunks, SPAN, STATE)
        c_act = a[:, DI + STATE :].reshape(chunks, SPAN, STATE)
        gc_state = gc_state + jnp.einsum(
            "gts,gsn->gtn", gcb_b, b_act, preferred_element_type=f32
        ).reshape(rows, STATE)
        gb = gb + jnp.einsum(
            "gts,gtn->gsn", gcb_b, c_act, preferred_element_type=f32
        ).reshape(rows, STATE)

        tail_sum = w * dw
        through = jnp.exp(last) * jnp.sum(cross, axis=2, keepdims=True)
        later = row_pair - dt * col_pair + carry - tail_sum
        glam = jnp.einsum("ght,st->ghs", later, upper, precision=highest)
        glam = glam + jnp.sum(tail_sum, axis=2, keepdims=True) + through
        gdt = col_pair + jnp.exp(last - cum) * dw + rate[:, None] * glam
        gr = gdt * jax.nn.sigmoid(pre)
        grad_heads = jnp.stack(
            [
                jnp.sum(gr, axis=(0, 2)),
                jnp.sum(glam * lam, axis=(0, 2)),
                jnp.sum(gskip, axis=(0, 2)),
            ]
        )
        gr_tok = gr.transpose(0, 2, 1).reshape(rows, H).astype(bf16)

        ga = jnp.concatenate([gx, gb, gc_state], axis=1)
        gpa = (ga * silu_slope(pa)).reshape(seqs, toks, CH)
        halo = lax.ppermute(gpa[:, :rim, :], "seq", left)
        gpad = jnp.concatenate([gpa, halo], axis=1)
        gc = jnp.zeros((), f32)
        grad_taps = []
        for k in range(TAPS):
            gc = gc + gpad[:, rim - k : rim - k + toks, :] * taps[k]
            grad_taps.append(jnp.sum(gpa * padded[:, k : k + toks, :].astype(f32), axis=(0, 1)))
        grad_taps.append(jnp.sum(gpa, axis=(0, 1)))
        gproj = jnp.concatenate([gz, gc.reshape(rows, CH).astype(bf16), gr_tok], axis=1)
        gu = dot(gproj, in_mats[i], 1, 1)
        grad_in = dot(u, gproj, 0, 0).astype(bf16)
        grad_in = lax.psum_scatter(grad_in, "fsdp", scatter_dimension=0, tiled=True)
        grad_in = lax.psum(grad_in, "seq").astype(f32)
        v = gu * g1
        mean_vh = jnp.mean(v * h, axis=-1, keepdims=True)
        grad_g1 = jnp.sum(gu * h * rs1, axis=0)
        grad = grad + rs1 * v - h * (rs1 * rs1 * rs1) * mean_vh
        big_grads[i] = (grad_in, grad_out)
        small_grads[i] = jnp.concatenate(
            [grad_g1, grad_g2, jnp.stack(grad_taps).reshape(-1), grad_heads.reshape(-1)]
        )

    small = lax.psum(jnp.stack(small_grads), ("seq", "fsdp"))
    size_a = D + DI
    size_b = size_a + (TAPS + 1) * CH
    own_gains = gains.shape[1]
    own_taps = conv_taps.shape[2]
    own_heads = head_params.shape[2]
    grads = (
        lax.dynamic_slice_in_dim(small[:, :size_a], fsdp_index * own_gains, own_gains, 1),
        jnp.stack([g[0] for g in big_grads]),
        lax.dynamic_slice_in_dim(
            small[:, size_a:size_b].reshape(LAYERS, TAPS + 1, CH), fsdp_index * own_taps, own_taps, 2
        ),
        lax.dynamic_slice_in_dim(
            small[:, size_b:].reshape(LAYERS, 3, H), fsdp_index * own_heads, own_heads, 2
        ),
        jnp.stack([g[1] for g in big_grads]),
    )
    results = [hidden.reshape(seqs, toks, D), grad.reshape(seqs, toks, D)]
    for kind in range(5):
        results.extend(
            adam_step(
                masters[kind], firsts[kind], seconds[kind], grads[kind],
                learn_rates[kind], weight_decays[kind],
            )
        )
    return tuple(results)


def solution(mesh):
    tokens = P("fsdp", "seq", None)
    per_kind = (P(None, "fsdp"), P(None, "fsdp", None), P(None, None, "fsdp"), P(None, None, "fsdp"), P(None, "fsdp", None))
    specs = (tokens, tokens) + tuple(s for s in per_kind for _ in range(3))
    return jax.shard_map(local, mesh=mesh, in_specs=specs, out_specs=specs, check_vma=False)
```

```python
import functools

import jax
import jax.numpy as jnp
from jax import lax
from jax.experimental import pallas as pl
from jax.experimental.pallas import tpu as pltpu
from jax.sharding import PartitionSpec as P

D = 1024
H = 32
HP = 64
STATE = 128
TAPS = 4
SPAN = 256
LAYERS = 2
STEP = 10
DI = 2048
CH = 2304
GROUP = 8
COLS = GROUP * HP

highest = lax.Precision.HIGHEST
norm_eps = 1e-05
beta_one = 0.9
beta_two = 0.95
adam_eps = 1e-08
learn_rates = (0.4, 0.06, 0.5, 3.0, 0.05)
weight_decays = (0.0, 0.1, 0.0, 0.0, 0.1)
bf16 = jnp.bfloat16
f32 = jnp.float32


def dot(a, b, ca, cb):
    return lax.dot_general(a, b, (((ca,), (cb,)), ((), ())), preferred_element_type=f32)


def head(ref, j):
    return ref[:, j * HP : (j + 1) * HP]


def state_kernel(x_ref, b_ref, w_ref, s_ref):
    w = jnp.transpose(w_ref[0])
    for j in range(GROUP):
        wx = (head(x_ref, j).astype(f32) * w[:, j : j + 1]).astype(bf16)
        s_ref[0, j * HP : (j + 1) * HP, :] = dot(wx, b_ref[...], 0, 0).astype(bf16)


def decay(cum, cum_cols, j, causal):
    gaps = cum_cols[:, j : j + 1] - cum[j : j + 1, :]
    return jnp.exp(jnp.where(causal, gaps, -1e30))


def causal_mask():
    rows = lax.broadcasted_iota(jnp.int32, (SPAN, SPAN), 0)
    cols = lax.broadcasted_iota(jnp.int32, (SPAN, SPAN), 1)
    return rows >= cols


def inner_kernel(x_ref, b_ref, c_ref, cum_ref, dt_ref, y_ref):
    causal = causal_mask()
    cb = dot(c_ref[...], b_ref[...], 1, 1)
    cum = cum_ref[0]
    dt = dt_ref[0]
    cum_cols = jnp.transpose(cum)
    for j in range(GROUP):
        mix = decay(cum, cum_cols, j, causal) * cb * dt[j : j + 1, :]
        y_ref[:, j * HP : (j + 1) * HP] = dot(mix.astype(bf16), head(x_ref, j), 1, 0)


def carry_kernel(y_ref, x_ref, c_ref, cum_ref, skip_ref, hin_ref, out_ref):
    grow = jnp.transpose(jnp.exp(cum_ref[0]))
    skip = jnp.transpose(skip_ref[0])
    for j in range(GROUP):
        rows = slice(j * HP, (j + 1) * HP)
        from_carry = dot(c_ref[...], hin_ref[0, rows, :], 1, 1) * grow[:, j : j + 1]
        skipped = head(x_ref, j).astype(f32) * skip[:, j : j + 1]
        out_ref[:, rows] = (y_ref[:, rows] + from_carry + skipped).astype(bf16)


def back_state_kernel(gy_ref, c_ref, cum_ref, g_ref):
    grow = jnp.transpose(jnp.exp(cum_ref[0]))
    for j in range(GROUP):
        egy = (head(gy_ref, j).astype(f32) * grow[:, j : j + 1]).astype(bf16)
        g_ref[0, j * HP : (j + 1) * HP, :] = dot(egy, c_ref[...], 0, 0).astype(bf16)


def back_inner_kernel(
    x_ref, gy_ref, b_ref, c_ref, cum_ref, dt_ref, skip_ref,
    gx_ref, gcb_ref, row_ref, col_ref, gskip_ref,
):
    causal = causal_mask()
    cb = dot(c_ref[...], b_ref[...], 1, 1)
    cum = cum_ref[0]
    dt = dt_ref[0]
    cum_cols = jnp.transpose(cum)
    dt_cols = jnp.transpose(dt)
    skip = jnp.transpose(skip_ref[0])

    @pl.when(pl.program_id(1) == 0)
    def _():
        gcb_ref[...] = jnp.zeros_like(gcb_ref)

    total = jnp.zeros((SPAN, SPAN), f32)
    row_list, skip_list = [], []
    for j in range(GROUP):
        e = decay(cum, cum_cols, j, causal)
        x = head(x_ref, j)
        gy = head(gy_ref, j)
        rho = dot(gy, x, 1, 1)
        e_rho = e * rho
        kept = e_rho * dt[j : j + 1, :]
        total = total + kept
        row_list.append(jnp.sum(kept * cb, axis=1, keepdims=True))
        col_ref[0, j : j + 1, :] = jnp.sum(e_rho * cb, axis=0, keepdims=True)
        gx = dot((e * cb).astype(bf16), gy, 0, 0) * dt_cols[:, j : j + 1]
        gyf = gy.astype(f32)
        gx_ref[:, j * HP : (j + 1) * HP] = gx + gyf * skip[:, j : j + 1]
        skip_list.append(jnp.sum(gyf * x.astype(f32), axis=1, keepdims=True))
    gcb_ref[0] += total
    row_ref[0] = jnp.transpose(jnp.concatenate(row_list, axis=1))
    gskip_ref[0] = jnp.transpose(jnp.concatenate(skip_list, axis=1))


def back_carry_kernel(
    gxi_ref, x_ref, gy_ref, b_ref, c_ref, cum_ref, w_ref, hin_ref, gs_ref,
    gx_ref, gb_ref, gc_ref, carry_ref, dw_ref, cross_ref,
):
    @pl.when(pl.program_id(1) == 0)
    def _():
        gb_ref[...] = jnp.zeros_like(gb_ref)
        gc_ref[...] = jnp.zeros_like(gc_ref)

    grow = jnp.transpose(jnp.exp(cum_ref[0]))
    w = jnp.transpose(w_ref[0])
    gb = jnp.zeros((SPAN, STATE), f32)
    gc = jnp.zeros((SPAN, STATE), f32)
    carry_list, dw_list = [], []
    for j in range(GROUP):
        rows = slice(j * HP, (j + 1) * HP)
        hin = hin_ref[0, rows, :]
        gs = gs_ref[0, rows, :]
        x = head(x_ref, j).astype(f32)
        egy = head(gy_ref, j).astype(f32) * grow[:, j : j + 1]
        b_gs = dot(b_ref[...], gs, 1, 1)
        c_hin = dot(c_ref[...], hin, 1, 1)
        gx_ref[:, rows] = gxi_ref[:, rows] + b_gs * w[:, j : j + 1]
        dw_list.append(jnp.sum(x * b_gs, axis=1, keepdims=True))
        carry_list.append(jnp.sum(egy * c_hin, axis=1, keepdims=True))
        gb = gb + dot((x * w[:, j : j + 1]).astype(bf16), gs, 1, 0)
        gc = gc + dot(egy.astype(bf16), hin, 1, 0)
        cross_ref[0, j : j + 1, :] = jnp.sum(hin.astype(f32) * gs.astype(f32), axis=0, keepdims=True)
    gb_ref[...] += gb
    gc_ref[...] += gc
    carry_ref[0] = jnp.transpose(jnp.concatenate(carry_list, axis=1))
    dw_ref[0] = jnp.transpose(jnp.concatenate(dw_list, axis=1))


x_spec = pl.BlockSpec((SPAN, COLS), lambda g, i: (g, i))
b_spec = pl.BlockSpec((SPAN, STATE), lambda g, i: (g, DI // STATE))
c_spec = pl.BlockSpec((SPAN, STATE), lambda g, i: (g, DI // STATE + 1))
bc_out_spec = pl.BlockSpec((SPAN, STATE), lambda g, i: (g, 0))
row_spec = pl.BlockSpec((1, GROUP, SPAN), lambda g, i: (g, i, 0))
one_spec = pl.BlockSpec((1, GROUP, 1), lambda g, i: (0, i, 0))
state_spec = pl.BlockSpec((1, COLS, STATE), lambda g, i: (g, i, 0))
gcb_spec = pl.BlockSpec((1, SPAN, SPAN), lambda g, i: (g, 0, 0))
cross_spec = pl.BlockSpec((1, GROUP, STATE), lambda g, i: (g, i, 0))


def call(kernel, name, chunks, ins, outs, flops, *args):
    shapes = [s for _, s in outs]
    moved = sum(a.size * a.dtype.itemsize for a in args)
    moved += sum(s.size * s.dtype.itemsize for s in shapes)
    return pl.pallas_call(
        kernel,
        grid=(chunks, H // GROUP),
        in_specs=ins,
        out_specs=[s for s, _ in outs],
        out_shape=shapes,
        name=name,
        compiler_params=pltpu.CompilerParams(
            dimension_semantics=("arbitrary", "arbitrary"), vmem_limit_bytes=40 * 1024 * 1024
        ),
        cost_estimate=pl.CostEstimate(
            flops=flops * chunks, bytes_accessed=moved, transcendentals=chunks * H * SPAN * SPAN
        ),
    )(*args)


def shape(dims, dtype=f32):
    return jax.ShapeDtypeStruct(dims, dtype)


small_flops = 2 * SPAN * DI * STATE
inner_flops = 20 * H * SPAN * SPAN * HP


def rms_scale(values):
    return lax.rsqrt(jnp.mean(values * values, axis=-1, keepdims=True) + norm_eps)


def silu_slope(w):
    sig = jax.nn.sigmoid(w)
    return sig * (1.0 + w * (1.0 - sig))


def adam_step(weight, first_old, second_old, grad_vals, learn_rate, decay_rate):
    first_new = beta_one * first_old + (1.0 - beta_one) * grad_vals
    second_new = beta_two * second_old + (1.0 - beta_two) * grad_vals * grad_vals
    first_hat = first_new / (1.0 - beta_one**STEP)
    second_hat = second_new / (1.0 - beta_two**STEP)
    weight_new = weight - learn_rate * (
        first_hat / (jnp.sqrt(second_hat) + adam_eps) + decay_rate * weight
    )
    return (first_new, second_new, weight_new)


def exchange(states, seqs, weights, shards, spec):
    n = states.shape[0] // seqs
    own = DI // shards
    send = states.reshape(seqs * n, shards, own, STATE)
    got = lax.all_to_all(send, "seq", split_axis=1, concat_axis=0, tiled=False)
    got = got.reshape(shards, seqs, n, own // HP, HP * STATE)
    got = got.astype(f32)
    mixed = jnp.einsum(spec, weights, got, precision=highest).astype(bf16)
    mixed = mixed.reshape(shards, seqs * n, own, STATE)
    back = lax.all_to_all(mixed, "seq", split_axis=0, concat_axis=1, tiled=False)
    return back.reshape(seqs * n, DI, STATE)


def chunk_weights(totals, seqs, shards):
    n = totals.shape[0] // seqs
    chunks = shards * n
    own = H // shards
    mine = lax.all_to_all(
        totals.reshape(seqs, n, H), "seq", split_axis=2, concat_axis=1, tiled=True
    )
    place = jnp.arange(chunks)
    between = (place[None, None, :] < place[:, None, None]) & (place[None, None, :] > place[None, :, None])
    logs = jnp.einsum("ijk,bkh->ijbh", between.astype(f32), mine, precision=highest)
    ahead = (place[:, None] > place[None, :])[:, :, None, None]
    weights = jnp.where(ahead, jnp.exp(jnp.where(ahead, logs, 0.0)), 0.0)
    return weights.reshape(shards, n, shards, n, seqs, own)


def local(
    hidden_in,
    cotangent,
    gains,
    gains_first,
    gains_second,
    in_proj,
    in_proj_first,
    in_proj_second,
    conv_taps,
    conv_taps_first,
    conv_taps_second,
    head_params,
    head_params_first,
    head_params_second,
    out_proj,
    out_proj_first,
    out_proj_second,
):
    masters = (gains, in_proj, conv_taps, head_params, out_proj)
    firsts = (gains_first, in_proj_first, conv_taps_first, head_params_first, out_proj_first)
    seconds = (gains_second, in_proj_second, conv_taps_second, head_params_second, out_proj_second)
    shards = lax.axis_size("seq")
    owners = lax.axis_size("fsdp")
    seqs, toks, _ = hidden_in.shape
    rows = seqs * toks
    n = toks // SPAN
    chunks = seqs * n
    rim = TAPS - 1
    right = [(i, i + 1) for i in range(shards - 1)]
    left = [(i + 1, i) for i in range(shards - 1)]

    smalls = jnp.concatenate(
        [gains.reshape(-1), conv_taps.reshape(-1), head_params.reshape(-1)]
    ).astype(bf16)
    smalls = lax.all_gather(smalls, "fsdp", axis=0)
    size_a = gains.size
    size_b = size_a + conv_taps.size
    gains_all = smalls[:, :size_a].reshape(owners, LAYERS, -1)
    gains_all = jnp.moveaxis(gains_all, 0, 1).reshape(LAYERS, D + DI).astype(f32)
    taps_all = smalls[:, size_a:size_b].reshape(owners, LAYERS, TAPS + 1, -1)
    taps_all = jnp.moveaxis(taps_all, 0, 2).reshape(LAYERS, TAPS + 1, CH).astype(f32)
    heads_all = smalls[:, size_b:].reshape(owners, LAYERS, 3, -1)
    heads_all = jnp.moveaxis(heads_all, 0, 2).reshape(LAYERS, 3, H).astype(f32)
    in_mats = [
        lax.all_gather(in_proj[i].astype(bf16), "fsdp", axis=0, tiled=True) for i in range(LAYERS)
    ]
    out_mats = [
        lax.all_gather(out_proj[i].astype(bf16), "fsdp", axis=0, tiled=True) for i in range(LAYERS)
    ]

    upper = (jnp.arange(SPAN)[:, None] <= jnp.arange(SPAN)[None, :]).astype(f32)

    hidden = hidden_in.astype(f32).reshape(rows, D)
    saved = []
    for i in range(LAYERS):
        g1, g2 = gains_all[i, :D], gains_all[i, D:]
        taps, heads = taps_all[i], heads_all[i]
        rs1 = rms_scale(hidden)
        u = (hidden * rs1 * g1).astype(bf16)
        proj = dot(u, in_mats[i], 1, 0).astype(bf16)
        z = proj[:, :DI]
        c = proj[:, DI : DI + CH].reshape(seqs, toks, CH)
        raw = proj[:, DI + CH :].astype(f32).reshape(chunks, SPAN, H).transpose(0, 2, 1)
        halo = lax.ppermute(c[:, toks - rim :, :], "seq", right)
        padded = jnp.concatenate([halo, c], axis=1)
        pa = taps[TAPS]
        for k in range(TAPS):
            pa = pa + padded[:, k : k + toks, :].astype(f32) * taps[k]
        pa = pa.reshape(rows, CH)
        a = (pa * jax.nn.sigmoid(pa)).astype(bf16)
        pre = raw + heads[0][:, None]
        dt = jax.nn.softplus(pre)
        rate = -jnp.exp(heads[1])
        lam = rate[:, None] * dt
        cum = jnp.einsum("ghs,st->ght", lam, upper, precision=highest)
        last = cum[:, :, SPAN - 1 :]
        tail = jnp.exp(last - cum)
        w = tail * dt
        skip = heads[2].reshape(1, H, 1)
        (state,) = call(
            state_kernel, "chunk_state", chunks, [x_spec, b_spec, row_spec],
            [(state_spec, shape((chunks, DI, STATE), bf16))], small_flops, a, a, w,
        )
        weights = chunk_weights(last[:, :, 0], seqs, shards)
        hin = exchange(state, seqs, weights, shards, "imjnbh,jbnhx->ibmhx")
        (inner,) = call(
            inner_kernel, "inner", chunks, [x_spec, b_spec, c_spec, row_spec, row_spec],
            [(x_spec, shape((rows, DI)))], inner_flops // 3, a, a, a, cum, dt,
        )
        (y,) = call(
            carry_kernel, "carry", chunks,
            [x_spec, x_spec, c_spec, row_spec, one_spec, state_spec],
            [(x_spec, shape((rows, DI), bf16))], small_flops, inner, a, a, cum, skip, hin,
        )
        yf, zf = y.astype(f32), z.astype(f32)
        q = yf * (zf * jax.nn.sigmoid(zf))
        rs2 = rms_scale(q)
        nrm = (q * rs2 * g2).astype(bf16)
        saved.append((hidden, rs1, u, y, z, padded, pa, a, pre, dt, lam, rate, cum, last, w, skip, weights, hin, rs2, nrm))
        hidden = hidden + dot(nrm, out_mats[i], 1, 0)

    grad = cotangent.reshape(rows, D)
    big_grads = [None] * LAYERS
    small_grads = [None] * LAYERS
    before = None
    for i in reversed(range(LAYERS)):
        (h, rs1, u, y, z, padded, pa, a, pre, dt, lam, rate, cum, last, w, skip, weights, hin, rs2, nrm) = saved[i]
        g1, g2 = gains_all[i, :D], gains_all[i, D:]
        taps = taps_all[i]
        go = grad.astype(bf16)
        gn = dot(go, out_mats[i], 1, 1)
        yf, zf = y.astype(f32), z.astype(f32)
        gate = zf * jax.nn.sigmoid(zf)
        q = yf * gate
        v = gn * g2
        gq = rs2 * v - q * (rs2 * rs2 * rs2) * jnp.mean(v * q, axis=-1, keepdims=True)
        grad_g2 = jnp.sum(gn * q * rs2, axis=0)
        gz = (gq * yf * silu_slope(zf)).astype(bf16)
        gy = (gq * gate).astype(bf16)
        (gstate,) = call(
            back_state_kernel, "back_state", chunks, [x_spec, c_spec, row_spec],
            [(state_spec, shape((chunks, DI, STATE), bf16))], small_flops, gy, a, cum,
        )
        gs = exchange(gstate, seqs, weights, shards, "imjnbh,ibmhx->jbnhx")
        grad_out = dot(nrm, go, 0, 0).astype(bf16)
        grad_out = lax.psum_scatter(grad_out, "fsdp", scatter_dimension=0, tiled=True)
        grad_gate = dot(u, gz, 0, 0).astype(bf16)
        grad_gate = lax.psum_scatter(grad_gate, "fsdp", scatter_dimension=0, tiled=True)
        if before is not None:
            grad_out, grad_gate, before = lax.optimization_barrier((grad_out, grad_gate, before))
            big_grads[i + 1] += (before,)
        grad_out, grad_gate = lax.psum((grad_out, grad_gate), "seq")
        rows_shape = shape((chunks, H, SPAN))
        gx, gcb, row_pair, col_pair, gskip = call(
            back_inner_kernel, "back_inner", chunks,
            [x_spec, x_spec, b_spec, c_spec, row_spec, row_spec, one_spec],
            [
                (x_spec, shape((rows, DI))), (gcb_spec, shape((chunks, SPAN, SPAN))),
                (row_spec, rows_shape), (row_spec, rows_shape), (row_spec, rows_shape),
            ],
            inner_flops, a, gy, a, a, cum, dt, skip,
        )
        gx, gb, gc_state, carry, dw, cross = call(
            back_carry_kernel, "back_carry", chunks,
            [x_spec, x_spec, x_spec, b_spec, c_spec, row_spec, row_spec, state_spec, state_spec],
            [
                (x_spec, shape((rows, DI))), (bc_out_spec, shape((rows, STATE))),
                (bc_out_spec, shape((rows, STATE))), (row_spec, rows_shape), (row_spec, rows_shape),
                (cross_spec, shape((chunks, H, STATE))),
            ],
            4 * small_flops, gx, a, gy, a, a, cum, w, hin, gs,
        )
        gcb_b = gcb.astype(bf16)
        b_act = a[:, DI : DI + STATE].reshape(chunks, SPAN, STATE)
        c_act = a[:, DI + STATE :].reshape(chunks, SPAN, STATE)
        gc_state = gc_state + jnp.einsum(
            "gts,gsn->gtn", gcb_b, b_act, preferred_element_type=f32
        ).reshape(rows, STATE)
        gb = gb + jnp.einsum(
            "gts,gtn->gsn", gcb_b, c_act, preferred_element_type=f32
        ).reshape(rows, STATE)

        tail_sum = w * dw
        through = jnp.exp(last) * jnp.sum(cross, axis=2, keepdims=True)
        later = row_pair - dt * col_pair + carry - tail_sum
        glam = jnp.einsum("ght,st->ghs", later, upper, precision=highest)
        glam = glam + jnp.sum(tail_sum, axis=2, keepdims=True) + through
        gdt = col_pair + jnp.exp(last - cum) * dw + rate[:, None] * glam
        gr = gdt * jax.nn.sigmoid(pre)
        grad_heads = jnp.stack(
            [
                jnp.sum(gr, axis=(0, 2)),
                jnp.sum(glam * lam, axis=(0, 2)),
                jnp.sum(gskip, axis=(0, 2)),
            ]
        )
        gr_tok = gr.transpose(0, 2, 1).reshape(rows, H).astype(bf16)

        ga = jnp.concatenate([gx, gb, gc_state], axis=1)
        gpa = (ga * silu_slope(pa)).reshape(seqs, toks, CH)
        halo = lax.ppermute(gpa[:, :rim, :], "seq", left)
        gpad = jnp.concatenate([gpa, halo], axis=1)
        gc = jnp.zeros((), f32)
        grad_taps = []
        for k in range(TAPS):
            gc = gc + gpad[:, rim - k : rim - k + toks, :] * taps[k]
            grad_taps.append(jnp.sum(gpa * padded[:, k : k + toks, :].astype(f32), axis=(0, 1)))
        grad_taps.append(jnp.sum(gpa, axis=(0, 1)))
        gscan = jnp.concatenate([gc.reshape(rows, CH).astype(bf16), gr_tok], axis=1)
        grad_in = dot(u, gscan, 0, 0).astype(bf16)
        grad_in = lax.psum_scatter(grad_in, "fsdp", scatter_dimension=0, tiled=True)
        grad_in, grad_out, grad_gate = lax.optimization_barrier((grad_in, grad_out, grad_gate))
        before = lax.psum(grad_in, "seq")
        gu = dot(jnp.concatenate([gz, gscan], axis=1), in_mats[i], 1, 1)
        v = gu * g1
        mean_vh = jnp.mean(v * h, axis=-1, keepdims=True)
        grad_g1 = jnp.sum(gu * h * rs1, axis=0)
        grad = grad + rs1 * v - h * (rs1 * rs1 * rs1) * mean_vh
        big_grads[i] = (grad_out, grad_gate)
        small_grads[i] = jnp.concatenate(
            [grad_g1, grad_g2, jnp.stack(grad_taps).reshape(-1), grad_heads.reshape(-1)]
        )

    big_grads[0] += (before,)
    small = jnp.stack(small_grads)
    size_a = D + DI
    size_b = size_a + (TAPS + 1) * CH

    def by_owner(part):
        part = part.reshape(part.shape[:-1] + (owners, part.shape[-1] // owners))
        return jnp.moveaxis(part, -2, 0).reshape(owners, -1)

    pieces = jnp.concatenate(
        [
            by_owner(small[:, :size_a]),
            by_owner(small[:, size_a:size_b].reshape(LAYERS, TAPS + 1, CH)),
            by_owner(small[:, size_b:].reshape(LAYERS, 3, H)),
        ],
        axis=1,
    )
    pieces = jnp.sum(lax.all_to_all(pieces, "fsdp", split_axis=0, concat_axis=0, tiled=True), axis=0)
    pieces = jnp.broadcast_to(pieces, (shards,) + pieces.shape)
    pieces = jnp.sum(lax.all_to_all(pieces, "seq", split_axis=0, concat_axis=0, tiled=True), axis=0)
    size_a = gains.size
    size_b = size_a + conv_taps.size
    grads = (
        pieces[:size_a].reshape(gains.shape),
        jnp.stack([jnp.concatenate(g[1:], axis=1) for g in big_grads]).astype(f32),
        pieces[size_a:size_b].reshape(conv_taps.shape),
        pieces[size_b:].reshape(head_params.shape),
        jnp.stack([g[0] for g in big_grads]).astype(f32),
    )
    results = [hidden.reshape(seqs, toks, D), grad.reshape(seqs, toks, D)]
    for kind in range(5):
        results.extend(
            adam_step(
                masters[kind], firsts[kind], seconds[kind], grads[kind],
                learn_rates[kind], weight_decays[kind],
            )
        )
    return tuple(results)


def solution(mesh):
    tokens = P("fsdp", "seq", None)
    per_kind = (P(None, "fsdp"), P(None, "fsdp", None), P(None, None, "fsdp"), P(None, None, "fsdp"), P(None, "fsdp", None))
    specs = (tokens, tokens) + tuple(s for s in per_kind for _ in range(3))
    return jax.shard_map(local, mesh=mesh, in_specs=specs, out_specs=specs, check_vma=False)
```
